32 devices in a mesh: parts: 2 (over y), blk: 4 (over z), grp: 4 (over x, core).
Axes of the slice: x: 2, y: 2, z: 4, core: 2. Of those that a mesh axis runs over, the one named last changes fastest.
Arguments:
- node_feats: bfloat16 [16384, 256], P(('parts', 'blk', 'grp')), parts along dimension 0, may hold values from -6 to 6
- mean_feats: bfloat16 [16384, 256], P(('parts', 'blk', 'grp')), parts along dimension 0, may hold values from -6 to 6
- cotangent: bfloat16 [16384, 256], P(('parts', 'blk', 'grp')), parts along dimension 0, may hold values from -6 to 6
- w_self: bfloat16 [256, 256], replicated, may hold values from -0.375 to 0.375
- w_neigh: bfloat16 [256, 256], replicated, may hold values from -0.375 to 0.375
- degree: int32 [16384], P(('parts', 'blk', 'grp')), parts along dimension 0, may hold values from 1 to 32
- adjacency: bfloat16 [8, 4, 4, 6, 128, 128], P(('parts', 'blk'), 'grp'), parts along dimension 0, may hold values from 0 to 1, as said below
- dst_tiles: int32 [8, 4, 4, 6], P(('parts', 'blk'), 'grp'), parts along dimension 0, may hold values from 0 to 15
- src_tiles: int32 [8, 4, 4, 6], P(('parts', 'blk'), 'grp'), parts along dimension 0, may hold values from 0 to 3
- tile_counts: int32 [8, 4, 4], P(('parts', 'blk'), 'grp'), parts along dimension 0, may hold values from 1 to 6, as said below
Outputs:
- grad_input: bfloat16 [16384, 256], P(('parts', 'blk', 'grp')), parts along dimension 0
- grad_self: float32 [512, 256], P('parts'), parts along dimension 0
- grad_neigh: float32 [512, 256], P('parts'), parts along dimension 0
The draws below stay inside these ranges and needn't reach their ends.
There are 2 independent parts, one for each index of `parts`. The reference program is written for one: setup_inputs(seed, part) draws one part's arguments, and reference() takes and returns one part's arrays. A program takes and returns all parts, laid end to end along the dimension named above; an argument that names none is the same for every part. Nothing has to cross between parts.
Inputs may be any that keep to these rules, and one draw needn't show every extreme that they name: `tile_counts`: every holder has at least one live slot for every source row group; some holder fills all 6 slots for some source row group in every draw. `adjacency`: entries are 0 or 1.
All inputs are finite; a program needn't handle non-finite values.
Results may differ from the reference program's by a relative error of at most 0.0046.
Values may be sent and summed in bfloat16 or wider, within the bound.
A program may use at most 128 MiB of HBM per device.

```python
import jax
import jax.numpy as jnp
from jax import lax

F = 256
TILE = 128
SLOTS = 6
DEV_TILES = 4
GROUP_TILES = 16
NODES = 8192
N_BLK = 4
N_GRP = 4


def draw_adjacency(key, part):
    key = jax.random.fold_in(key, 11)
    shape = (N_BLK, N_GRP, N_BLK, SLOTS, TILE, TILE)
    odds = 8
    picks = jax.random.randint(key, shape, 0, odds)
    return (picks == 0).astype(jnp.float32).astype(jnp.bfloat16)


def draw_dst_tiles(key, part):
    key = jax.random.fold_in(key, 12)
    return jax.random.randint(key, (N_BLK, N_GRP, N_BLK, SLOTS), 0, GROUP_TILES).astype(jnp.int32)


def draw_src_tiles(key, part):
    key = jax.random.fold_in(key, 13)
    return jax.random.randint(key, (N_BLK, N_GRP, N_BLK, SLOTS), 0, DEV_TILES).astype(jnp.int32)


def draw_tile_counts(key, part):
    key = jax.random.fold_in(key, 14)
    key_cap, key_cnt, key_pos = jax.random.split(key, 3)
    caps = jax.random.randint(key_cap, (N_BLK, N_GRP, 1), SLOTS // 2, SLOTS + 1)
    counts = 1 + jax.random.randint(key_cnt, (N_BLK, N_GRP, N_BLK), 0, SLOTS) % caps
    spot = jax.random.randint(key_pos, (), 0, N_BLK * N_GRP * N_BLK)
    flat = jnp.arange(N_BLK * N_GRP * N_BLK, dtype=jnp.int32).reshape(N_BLK, N_GRP, N_BLK)
    counts = jnp.where(flat == spot, SLOTS, counts)
    return counts.astype(jnp.int32)


def set_ends(result, own_key, least, high):
    shape = result.shape
    place = [jax.random.randint(jax.random.fold_in(own_key, axis), (), 0, shape[axis]) for axis in range(len(shape))]
    result = result.at[tuple(place)].set(least)
    longest = shape.index(max(shape))
    place[longest] = (place[longest] + 1) % shape[longest]
    return result.at[tuple(place)].set(high)


def block_levels(own_key, extent, shards, smallest, top_value):
    gain = 1.0
    for axis_at, shards_of in shards:
        heights = jax.random.uniform(jax.random.fold_in(jax.random.fold_in(own_key, 6), axis_at), (shards_of,), jnp.float32, smallest / len(shards), top_value / len(shards))
        gain = gain * jnp.repeat(jnp.exp(heights), extent[axis_at] // shards_of).reshape((-1,) + (1,) * (len(extent) - 1 - axis_at))
    return gain


def normal_values(stream_key, dims, scale, limit, shards=(), kind=jnp.bfloat16):
    array = jax.random.normal(stream_key, dims, jnp.float32) * scale
    if len(shards) > 0:
        array = block_levels(stream_key, dims, shards, -0.22, 0.18) * array
    return jnp.clip(array, min=-limit, max=limit).astype(kind)


def setup_inputs(seed: int = 0, part: int = 0) -> dict:
    splits = jax.random.split(jax.random.key(seed), 11)
    own_keys = jax.random.split(jax.random.fold_in(splits[10], part), 11)
    node_feats = normal_values(own_keys[0], (NODES, F), 1.0, 6.0, ((0, 16),))
    mean_feats = normal_values(own_keys[1], (NODES, F), 1.0, 6.0, ((0, 16),))
    cotangent = normal_values(own_keys[2], (NODES, F), 1.0, 6.0, ((0, 16),))
    w_self = normal_values(splits[3], (F, F), F ** -0.5, 0.375)
    w_neigh = normal_values(splits[4], (F, F), F ** -0.5, 0.375)
    degree = set_ends(jax.random.randint(own_keys[5], (NODES,), 1, 33), jax.random.fold_in(own_keys[5], 1), 1, 32).astype(jnp.int32)
    adjacency = draw_adjacency(jax.random.fold_in(jax.random.fold_in(splits[10], part), 71), part)
    dst_tiles = draw_dst_tiles(jax.random.fold_in(jax.random.fold_in(splits[10], part), 71), part)
    src_tiles = draw_src_tiles(jax.random.fold_in(jax.random.fold_in(splits[10], part), 71), part)
    tile_counts = draw_tile_counts(jax.random.fold_in(jax.random.fold_in(splits[10], part), 71), part)
    return dict(node_feats=node_feats, mean_feats=mean_feats, cotangent=cotangent, w_self=w_self, w_neigh=w_neigh, degree=degree, adjacency=adjacency, dst_tiles=dst_tiles, src_tiles=src_tiles, tile_counts=tile_counts)


def reference(node_feats, mean_feats, cotangent, w_self, w_neigh, degree, adjacency, dst_tiles, src_tiles, tile_counts):
    nodes = node_feats.shape[0]
    scaled = cotangent.astype(jnp.float32) / degree.astype(jnp.float32)[:, None]
    blocks = scaled.reshape(nodes // TILE, TILE, F)
    holders = N_BLK * N_GRP
    tiles_all = adjacency.reshape(holders, N_BLK, SLOTS, TILE, TILE)
    dst_all = dst_tiles.reshape(holders, N_BLK, SLOTS)
    src_all = src_tiles.reshape(holders, N_BLK, SLOTS)
    cnt_all = tile_counts.reshape(holders, N_BLK)
    source_rows = jnp.arange(N_BLK, dtype=jnp.int32)[:, None]
    slot_ids = jnp.arange(SLOTS, dtype=jnp.int32)[None, :]

    def one(holder, pulled_blocks):
        b_idx = (holder // N_GRP).astype(jnp.int32)
        g_idx = (holder % N_GRP).astype(jnp.int32)
        dst_glob = (b_idx * GROUP_TILES + dst_all[holder]).astype(jnp.int32)
        src_glob = ((source_rows * N_GRP + g_idx) * DEV_TILES + src_all[holder]).astype(jnp.int32)
        live = (slot_ids < cnt_all[holder][:, None]).astype(jnp.float32)
        rows = blocks[dst_glob]
        parts = jnp.einsum("stij,stif->stjf", tiles_all[holder].astype(jnp.float32), rows, precision=lax.Precision.HIGHEST)
        parts = parts * live[:, :, None, None]
        return pulled_blocks.at[src_glob].add(parts)

    pulled_blocks = lax.fori_loop(0, holders, one, jnp.zeros((nodes // TILE, TILE, F), jnp.float32))
    pulled_b = pulled_blocks.reshape(nodes, F).astype(jnp.bfloat16)
    grad_input = (jnp.dot(cotangent, w_self.T, preferred_element_type=jnp.float32) + jnp.dot(pulled_b, w_neigh.T, preferred_element_type=jnp.float32)).astype(jnp.bfloat16)
    factor = nodes ** -0.5
    grad_self = jnp.dot(node_feats.T, cotangent, preferred_element_type=jnp.float32) * factor
    grad_neigh = jnp.dot(mean_feats.T, cotangent, preferred_element_type=jnp.float32) * factor
    return grad_input, grad_self, grad_neigh
```

```python
import functools

import jax
import jax.numpy as jnp
from jax import lax
from jax.experimental import pallas as pl
from jax.experimental.pallas import tpu as pltpu
from jax.sharding import PartitionSpec as P

MESH = pl.DeviceIdType.MESH
F32, BF16 = jnp.float32, jnp.bfloat16
HALVES = 2


def kernel(
    dims,
    cot, node, mean, w_self, w_neigh, deg, adj, dst, src, cnt,
    gin, gself, gneigh,
    cot_v, node_v, mean_v, ws_v, wn_v, adj_v,
    cot_in0, cot_in1, deg_in, scaled0, scaled1, placed,
    part_out0, part_out1, part_in0, part_in1, acc0, acc1, own,
    w_acc, w_out, wz_in, wq, wg_in, zag, gag,
    load_sem, gs, gr, ds, dr, ps, pr_sem, zs, zr, qs, qr, as_, ar, bs, br,
):
    ng, nb, tile, slots, dev_tiles, rows, width, rq, pr, owners = dims
    half = width // HALVES
    g, b = lax.axis_index("grp"), lax.axis_index("blk")
    cot_in, scaled = (cot_in0, cot_in1), (scaled0, scaled1)
    part_out, part_in, acc = (part_out0, part_out1), (part_in0, part_in1), (acc0, acc1)

    loads = [
        pltpu.make_async_copy(a, v, load_sem.at[i])
        for i, (a, v) in enumerate(
            ((cot, cot_v), (node, node_v), (mean, mean_v), (adj, adj_v), (w_self, ws_v), (w_neigh, wn_v))
        )
    ]
    for c in loads:
        c.start()

    barrier = pltpu.get_barrier_semaphore()
    for d in range(1, ng):
        pl.semaphore_signal(barrier, inc=1, device_id={"grp": lax.rem(g + d, ng)}, device_id_type=MESH)
    for d in range(1, nb):
        pl.semaphore_signal(barrier, inc=1, device_id={"blk": lax.rem(b + d, nb)}, device_id_type=MESH)
    pl.semaphore_wait(barrier, ng - 1 + nb - 1)

    def deg_copy(d):
        return pltpu.make_async_remote_copy(
            src_ref=deg, dst_ref=deg_in.at[d - 1], send_sem=ds.at[d - 1], recv_sem=dr.at[d - 1],
            device_id={"grp": lax.rem(g + d, ng)}, device_id_type=MESH)

    def cot_copy(h, d):
        return pltpu.make_async_remote_copy(
            src_ref=cot.at[:, pl.ds(h * half, half)], dst_ref=cot_in[h].at[d - 1],
            send_sem=gs.at[h, d - 1], recv_sem=gr.at[h, d - 1],
            device_id={"grp": lax.rem(g + d, ng)}, device_id_type=MESH)

    for d in range(1, ng):
        deg_copy(d).start()
    for h in range(HALVES):
        for d in range(1, ng):
            cot_copy(h, d).start()

    for c in loads[:3]:
        c.wait()
    dims0 = (((0,), (0,)), ((), ()))
    for i, feats in enumerate((node_v, mean_v)):
        w = lax.dot_general(feats[...], cot_v[...], dims0, preferred_element_type=F32)
        w_acc[i * width:(i + 1) * width, :] = w
        w_out[i * width:(i + 1) * width, :] = w.astype(BF16)

    def wz_copy(d):
        to = lax.rem(b + d, nb)
        return pltpu.make_async_remote_copy(
            src_ref=w_out.at[pl.ds(pl.multiple_of(to * rq, rq), rq), :], dst_ref=wz_in.at[d - 1],
            send_sem=zs.at[d - 1], recv_sem=zr.at[d - 1],
            device_id={"blk": to}, device_id_type=MESH)

    for d in range(1, nb):
        wz_copy(d).start()

    loads[3].wait()

    def place(s, carry):
        for t in range(slots):
            turned = adj_v[0, 0, s, t].astype(F32).T
            live = t < cnt[0, 0, s]
            at = src[0, 0, s, t]
            for j in range(dev_tiles):
                keep = jnp.where(jnp.logical_and(live, at == j), 1.0, 0.0)
                placed[s, j * tile:(j + 1) * tile, t * tile:(t + 1) * tile] = (turned * keep).astype(BF16)
        return carry

    lax.fori_loop(0, nb, place, 0)

    loads[4].wait()
    loads[5].wait()
    dims1 = (((1,), (1,)), ((), ()))
    own[...] = lax.dot_general(cot_v[...], ws_v[...], dims1, preferred_element_type=F32)

    eye = lax.broadcasted_iota(jnp.int32, (tile, tile), 0) == lax.broadcasted_iota(jnp.int32, (tile, tile), 1)

    def scale(h, owner, values, degrees):
        for k in range(dev_tiles):
            line = jnp.broadcast_to(degrees[k:k + 1, :].astype(F32), (tile, tile))
            inv = 1.0 / jnp.sum(jnp.where(eye, line, 0.0), axis=1, keepdims=True)
            x = values[k * tile:(k + 1) * tile, :].astype(F32) * inv
            hi = x.astype(BF16)
            lo = (x - hi.astype(F32)).astype(BF16)
            scaled[h][owner * dev_tiles + k, :, 0:half] = hi
            scaled[h][owner * dev_tiles + k, :, half:2 * half] = lo

    def partial(h, to):
        picked = jnp.concatenate([scaled[h][dst[0, 0, to, t]] for t in range(slots)], axis=0)
        both = jnp.dot(placed[to], picked, preferred_element_type=F32)
        return both[:, :half] + both[:, half:]

    def part_copy(h, d):
        return pltpu.make_async_remote_copy(
            src_ref=part_out[h].at[d - 1], dst_ref=part_in[h].at[d - 1],
            send_sem=ps.at[h, d - 1], recv_sem=pr_sem.at[h, d - 1],
            device_id={"blk": lax.rem(b + d, nb)}, device_id_type=MESH)

    def wg_copy(d):
        to = lax.rem(g + d, ng)
        at = lax.rem(to, owners)
        return to, pltpu.make_async_remote_copy(
            src_ref=wq.at[pl.ds(pl.multiple_of(at * pr, pr), pr), :], dst_ref=wg_in.at[d - 1],
            send_sem=qs.at[d - 1], recv_sem=qr.at[d - 1],
            device_id={"grp": to}, device_id_type=MESH)

    def zag_copy(d):
        return pltpu.make_async_remote_copy(
            src_ref=zag.at[b], dst_ref=zag.at[b], send_sem=as_.at[d - 1], recv_sem=ar.at[d - 1],
            device_id={"blk": lax.rem(b + d, nb)}, device_id_type=MESH)

    def gag_copy(d):
        return pltpu.make_async_remote_copy(
            src_ref=zag, dst_ref=gag.at[d - 1], send_sem=bs.at[d - 1], recv_sem=br.at[d - 1],
            device_id={"grp": lax.rem(g + d, ng)}, device_id_type=MESH)

    for h in range(HALVES):
        scale(h, g, cot_v[:, h * half:(h + 1) * half], deg[...])
        for d in range(1, ng):
            if h == 0:
                deg_copy(d).wait_recv()
            cot_copy(h, d).wait_recv()
            scale(h, lax.rem(g - d + ng, ng), cot_in[h][d - 1], deg_in[d - 1])

        def send_part(d, carry, h=h):
            part_out[h][d - 1] = partial(h, lax.rem(b + d, nb)).astype(BF16)
            part_copy(h, d).start()
            return carry

        lax.fori_loop(1, nb, send_part, 0)
        acc[h][...] = partial(h, b)

        if h == 0:
            total = w_acc[pl.ds(pl.multiple_of(b * rq, rq), rq), :]
            for d in range(1, nb):
                wz_copy(d).wait_recv()
                total = total + wz_in[d - 1].astype(F32)
            wq[...] = total
            for d in range(1, ng):
                to, copy = wg_copy(d)
                pl.when(to < owners)(copy.start)

    factor = (rows * nb * ng) ** (-0.5)

    @pl.when(g < owners)
    def _():
        total = wq[pl.ds(pl.multiple_of(lax.rem(g, owners) * pr, pr), pr), :]
        for d in range(1, ng):
            wg_copy(d)[1].wait_recv()
            total = total + wg_in[d - 1]
        zag[b] = (total * factor).astype(BF16)
        for d in range(1, nb):
            zag_copy(d).start()
        for d in range(1, nb):
            zag_copy(d).wait_recv()
        for d in range(1, ng):
            gag_copy(d).start()

    pulled = []
    for h in range(HALVES):
        total = acc[h][...]
        for d in range(1, nb):
            part_copy(h, d).wait_recv()
            total = total + part_in[h][d - 1].astype(F32)
        pulled.append(total.astype(BF16))
    neigh = lax.dot_general(jnp.concatenate(pulled, axis=1), wn_v[...], dims1, preferred_element_type=F32)
    gin[...] = (own[...] + neigh).astype(BF16)

    def write(q, first, values):
        per = width // rq
        for out, base in ((gself, 0), (gneigh, per)):
            if q // per * per == base:
                out[pl.ds(pl.multiple_of((q - base) * rq + first, pr), pr), :] = values.astype(F32)

    @pl.when(g < owners)
    def _():
        for q in range(nb):
            write(q, lax.rem(g, owners) * pr, zag[q])

    for d in range(1, ng):
        owner = lax.rem(g - d + ng, ng)

        @pl.when(owner < owners)
        def _(d=d, owner=owner):
            gag_copy(d).wait_recv()
            for q in range(nb):
                write(q, lax.rem(owner, owners) * pr, gag[d - 1, q])

    for d in range(1, ng):
        deg_copy(d).wait_send()
        for h in range(HALVES):
            cot_copy(h, d).wait_send()
        to, copy = wg_copy(d)
        pl.when(to < owners)(copy.wait_send)
        pl.when(g < owners)(gag_copy(d).wait_send)
    for d in range(1, nb):
        wz_copy(d).wait_send()
        for h in range(HALVES):
            part_copy(h, d).wait_send()
        pl.when(g < owners)(zag_copy(d).wait_send)


def on_device(nb, ng, node_feats, mean_feats, cotangent, w_self, w_neigh, degree, adjacency, dst_tiles, src_tiles, tile_counts):
    rows, width = cotangent.shape
    tile, slots = adjacency.shape[-1], adjacency.shape[3]
    dev_tiles = rows // tile
    half = width // HALVES
    rq = 2 * width // nb
    pr = max(16, rq // ng)
    owners = rq // pr
    dims = (ng, nb, tile, slots, dev_tiles, rows, width, rq, pr, owners)
    any_spec = pl.BlockSpec(memory_space=pl.ANY)
    vmem, smem = pl.BlockSpec(memory_space=pltpu.VMEM), pl.BlockSpec(memory_space=pltpu.SMEM)
    dma = pltpu.SemaphoreType.DMA
    V = pltpu.VMEM
    return pl.pallas_call(
        functools.partial(kernel, dims),
        out_shape=(
            jax.ShapeDtypeStruct((rows, width), BF16),
            jax.ShapeDtypeStruct((width, width), F32),
            jax.ShapeDtypeStruct((width, width), F32),
        ),
        in_specs=[any_spec] * 5 + [vmem, any_spec] + [smem] * 3,
        out_specs=(vmem, vmem, vmem),
        scratch_shapes=[
            V((rows, width), BF16), V((rows, width), BF16), V((rows, width), BF16),
            V((width, width), BF16), V((width, width), BF16), V(adjacency.shape, BF16),
            V((ng - 1, rows, half), BF16), V((ng - 1, rows, half), BF16),
            V((ng - 1, dev_tiles, tile), jnp.int32),
            V((ng * dev_tiles, tile, width), BF16), V((ng * dev_tiles, tile, width), BF16),
            V((nb, rows, slots * tile), BF16),
            V((nb - 1, rows, half), BF16), V((nb - 1, rows, half), BF16),
            V((nb - 1, rows, half), BF16), V((nb - 1, rows, half), BF16),
            V((rows, half), F32), V((rows, half), F32), V((rows, width), F32),
            V((2 * width, width), F32), V((2 * width, width), BF16), V((nb - 1, rq, width), BF16),
            V((rq, width), F32), V((ng - 1, pr, width), F32),
            V((nb, pr, width), BF16), V((ng - 1, nb, pr, width), BF16),
            dma((6,)),
            dma((HALVES, ng - 1)), dma((HALVES, ng - 1)), dma((ng - 1,)), dma((ng - 1,)),
            dma((HALVES, nb - 1)), dma((HALVES, nb - 1)), dma((nb - 1,)), dma((nb - 1,)),
            dma((ng - 1,)), dma((ng - 1,)), dma((nb - 1,)), dma((nb - 1,)), dma((ng - 1,)), dma((ng - 1,)),
        ],
        compiler_params=pltpu.CompilerParams(
            collective_id=0, has_side_effects=True, vmem_limit_bytes=56 * 1024 * 1024
        ),
    )(
        cotangent, node_feats, mean_feats, w_self, w_neigh, degree.reshape(dev_tiles, tile),
        adjacency, dst_tiles, src_tiles, tile_counts,
    )


def solution(mesh):
    placed = (
        P(("parts", "blk", "grp"), None),
        P(("parts", "blk", "grp"), None),
        P(("parts", "blk", "grp"), None),
        P(),
        P(),
        P(("parts", "blk", "grp")),
        P(("parts", "blk"), "grp", None, None, None, None),
        P(("parts", "blk"), "grp", None, None),
        P(("parts", "blk"), "grp", None, None),
        P(("parts", "blk"), "grp", None),
    )
    return jax.shard_map(
        functools.partial(on_device, mesh.shape["blk"], mesh.shape["grp"]),
        mesh=mesh,
        in_specs=placed,
        out_specs=(P(("parts", "blk", "grp"), None), P("parts", None), P("parts", None)),
        check_vma=False,
    )
```

```python
import functools

import jax
import jax.numpy as jnp
from jax import lax
from jax.experimental import pallas as pl
from jax.experimental.pallas import tpu as pltpu
from jax.sharding import PartitionSpec as P

MESH = pl.DeviceIdType.MESH
F32, BF16 = jnp.float32, jnp.bfloat16
HALVES = 2


def kernel(
    dims,
    cot, node, mean, deg, adj, dst, src, cnt,
    pulled_b, w_sum,
    cot_v, node_v, mean_v, adj_v,
    cot_in0, cot_in1, deg_in, scaled0, scaled1, placed,
    part_out0, part_out1, part_in0, part_in1, acc0, acc1, relay_in,
    w_acc, w_out, wz_in, wq, wg_in, zag, gag,
    load_sem, gs, gr, ds, dr, ps, pr_sem, rr, zs, zr, qs, qr, as_, ar, bs, br,
):
    ng, nb, tile, slots, dev_tiles, rows, width, rq, pr, owners = dims
    half = width // HALVES
    relay = nb >= 4
    g, b = lax.axis_index("grp"), lax.axis_index("blk")
    cot_in, scaled = (cot_in0, cot_in1), (scaled0, scaled1)
    part_out, part_in, acc = (part_out0, part_out1), (part_in0, part_in1), (acc0, acc1)

    loads = [
        pltpu.make_async_copy(a, v, load_sem.at[i])
        for i, (a, v) in enumerate(
            ((cot, cot_v), (node, node_v), (mean, mean_v), (adj, adj_v))
        )
    ]
    for c in loads:
        c.start()

    barrier = pltpu.get_barrier_semaphore()
    for d in range(1, ng):
        pl.semaphore_signal(barrier, inc=1, device_id={"grp": lax.rem(g + d, ng)}, device_id_type=MESH)
    for d in range(1, nb):
        pl.semaphore_signal(barrier, inc=1, device_id={"blk": lax.rem(b + d, nb)}, device_id_type=MESH)
    pl.semaphore_wait(barrier, ng - 1 + nb - 1)

    def deg_copy(d):
        return pltpu.make_async_remote_copy(
            src_ref=deg, dst_ref=deg_in.at[d - 1], send_sem=ds.at[d - 1], recv_sem=dr.at[d - 1],
            device_id={"grp": lax.rem(g + d, ng)}, device_id_type=MESH)

    sib = g + 1 - 2 * lax.rem(g, 2)

    def cot_copy(h, d):
        to = sib if d == 0 else lax.rem(g + d, ng)
        return pltpu.make_async_remote_copy(
            src_ref=cot.at[:, pl.ds(h * half, half)], dst_ref=cot_in[h].at[g],
            send_sem=gs.at[h, 0, d // 2], recv_sem=gr.at[h, g],
            device_id={"grp": to}, device_id_type=MESH)

    def fwd_copy(h, d):
        owner = lax.rem(g - d + ng, ng)
        return pltpu.make_async_remote_copy(
            src_ref=cot_in[h].at[owner], dst_ref=cot_in[h].at[owner],
            send_sem=gs.at[h, 1, d // 2], recv_sem=gr.at[h, owner],
            device_id={"grp": sib}, device_id_type=MESH)

    def cot_arrival(h, owner):
        return pltpu.make_async_remote_copy(
            src_ref=cot_in[h].at[owner], dst_ref=cot_in[h].at[owner],
            send_sem=gs.at[h, 0, 0], recv_sem=gr.at[h, owner],
            device_id={"grp": sib}, device_id_type=MESH)

    for d in range(1, ng):
        deg_copy(d).start()
    for h in range(HALVES):
        for d in range(2, ng, 2):
            cot_copy(h, d).start()
        cot_copy(h, 0).start()

    for c in loads[:3]:
        c.wait()
    dims0 = (((0,), (0,)), ((), ()))
    for i, feats in enumerate((node_v, mean_v)):
        w = lax.dot_general(feats[...], cot_v[...], dims0, preferred_element_type=F32)
        w_acc[i * width:(i + 1) * width, :] = w
        w_out[i * width:(i + 1) * width, :] = w.astype(BF16)

    def wz_copy(d):
        to = lax.rem(b + d, nb)
        return pltpu.make_async_remote_copy(
            src_ref=w_out.at[pl.ds(pl.multiple_of(to * rq, rq), rq), :], dst_ref=wz_in.at[d - 1],
            send_sem=zs.at[d - 1], recv_sem=zr.at[d - 1],
            device_id={"blk": to}, device_id_type=MESH)

    for d in range(1, nb):
        wz_copy(d).start()

    loads[3].wait()

    def place(s, carry):
        for t in range(slots):
            turned = adj_v[0, 0, s, t].astype(F32).T
            live = t < cnt[0, 0, s]
            at = src[0, 0, s, t]
            for j in range(dev_tiles):
                keep = jnp.where(jnp.logical_and(live, at == j), 1.0, 0.0)
                placed[s, j * tile:(j + 1) * tile, t * tile:(t + 1) * tile] = (turned * keep).astype(BF16)
        return carry

    lax.fori_loop(0, nb, place, 0)

    eye = lax.broadcasted_iota(jnp.int32, (tile, tile), 0) == lax.broadcasted_iota(jnp.int32, (tile, tile), 1)

    def scale(h, owner, values, degrees):
        for k in range(dev_tiles):
            line = jnp.broadcast_to(degrees[k:k + 1, :].astype(F32), (tile, tile))
            inv = 1.0 / jnp.sum(jnp.where(eye, line, 0.0), axis=1, keepdims=True)
            x = values[k * tile:(k + 1) * tile, :].astype(F32) * inv
            hi = x.astype(BF16)
            lo = (x - hi.astype(F32)).astype(BF16)
            scaled[h][owner * dev_tiles + k, :, 0:half] = hi
            scaled[h][owner * dev_tiles + k, :, half:2 * half] = lo

    def partial(h, to):
        picked = jnp.concatenate([scaled[h][dst[0, 0, to, t]] for t in range(slots)], axis=0)
        both = jnp.dot(placed[to], picked, preferred_element_type=F32)
        return both[:, :half] + both[:, half:]

    def part_copy(h, d):
        return pltpu.make_async_remote_copy(
            src_ref=part_out[h].at[d - 1], dst_ref=part_in[h].at[d - 1],
            send_sem=ps.at[h, d - 1], recv_sem=pr_sem.at[h, d - 1],
            device_id={"blk": lax.rem(b + d, nb)}, device_id_type=MESH)

    def relay_copy(h, d):
        return pltpu.make_async_remote_copy(
            src_ref=part_out[h].at[d - 1], dst_ref=relay_in.at[h],
            send_sem=ps.at[h, d - 1], recv_sem=rr.at[h],
            device_id={"blk": 1 + (nb - 3) * (b // (nb - 1))}, device_id_type=MESH)

    def wg_copy(d):
        to = lax.rem(g + d, ng)
        at = lax.rem(to, owners)
        return to, pltpu.make_async_remote_copy(
            src_ref=wq.at[pl.ds(pl.multiple_of(at * pr, pr), pr), :], dst_ref=wg_in.at[d - 1],
            send_sem=qs.at[d - 1], recv_sem=qr.at[d - 1],
            device_id={"grp": to}, device_id_type=MESH)

    def zag_copy(d):
        return pltpu.make_async_remote_copy(
            src_ref=zag.at[b], dst_ref=zag.at[b], send_sem=as_.at[d - 1], recv_sem=ar.at[d - 1],
            device_id={"blk": lax.rem(b + d, nb)}, device_id_type=MESH)

    def gag_copy(d):
        return pltpu.make_async_remote_copy(
            src_ref=zag, dst_ref=gag.at[d - 1], send_sem=bs.at[d - 1], recv_sem=br.at[d - 1],
            device_id={"grp": lax.rem(g + d, ng)}, device_id_type=MESH)

    at_end = jnp.logical_or(b == 0, b == nb - 1)
    next_to_end = jnp.logical_or(b == 1, b == nb - 2)
    upper = b // (nb // 2)
    factor = (rows * nb * ng) ** (-0.5)

    for h in range(HALVES):
        scale(h, g, cot_v[:, h * half:(h + 1) * half], deg[...])
        if h == 0:
            for d in range(1, ng):
                deg_copy(d).wait_recv()

        def arrived(owner, h=h):
            scale(h, owner, cot_in[h][owner], deg_in[lax.rem(g - owner + ng, ng) - 1])

        for d in range(2, ng, 2):
            cot_arrival(h, lax.rem(g - d + ng, ng)).wait_recv()
            fwd_copy(h, d).start()
        cot_arrival(h, sib).wait_recv()
        arrived(sib)
        for d in range(2, ng, 2):
            arrived(lax.rem(g - d + ng, ng))
        for d in range(2, ng, 2):
            owner = lax.rem(sib - d + ng, ng)
            cot_arrival(h, owner).wait_recv()
            arrived(owner)

        def send_part(i, carry, h=h):
            d = lax.rem(i + nb - 2, nb - 1) + 1
            d = d * (1 - 2 * upper) + nb * upper
            value = partial(h, lax.rem(b + d, nb))
            if not relay:
                part_out[h][d - 1] = value.astype(BF16)
                part_copy(h, d).start()
                return carry
            far = jnp.logical_and(at_end, i == 0)
            join = jnp.logical_and(next_to_end, i == nb - 2)

            @pl.when(join)
            def _():
                relay_copy(h, d).wait_recv()
                part_out[h][d - 1] = (value + relay_in[h].astype(F32)).astype(BF16)

            @pl.when(jnp.logical_not(join))
            def _():
                part_out[h][d - 1] = value.astype(BF16)

            @pl.when(far)
            def _():
                relay_copy(h, d).start()

            @pl.when(jnp.logical_not(far))
            def _():
                part_copy(h, d).start()

            return carry

        if h == 1:
            @pl.when(g < owners)
            def _():
                total = wq[pl.ds(pl.multiple_of(lax.rem(g, owners) * pr, pr), pr), :]
                for d in range(1, ng):
                    wg_copy(d)[1].wait_recv()
                    total = total + wg_in[d - 1]
                zag[b] = (total * factor).astype(BF16)
                for d in range(1, nb):
                    zag_copy(d).start()

        lax.fori_loop(0, nb - 1, send_part, 0)
        acc[h][...] = partial(h, b)

        if h == 0:
            total = w_acc[pl.ds(pl.multiple_of(b * rq, rq), rq), :]
            for d in range(1, nb):
                wz_copy(d).wait_recv()
                total = total + wz_in[d - 1].astype(F32)
            wq[...] = total
            for d in range(1, ng):
                to, copy = wg_copy(d)
                pl.when(to < owners)(copy.start)

    def write(q, first, values):
        w_sum[pl.ds(pl.multiple_of(q * rq + first, pr), pr), :] = values

    def finish(h):
        for d in range(1, nb):
            def add(d=d):
                part_copy(h, d).wait_recv()
                acc[h][...] += part_in[h][d - 1].astype(F32)

            if relay and d == 1:
                pl.when(b != 0)(add)
            elif relay and d == nb - 1:
                pl.when(b != nb - 1)(add)
            else:
                add()
        pulled_b[:, h * half:(h + 1) * half] = acc[h][...].astype(BF16)

    @pl.when(g < owners)
    def _():
        for d in range(1, nb):
            zag_copy(d).wait_recv()
        for d in range(1, ng):
            gag_copy(d).start()
        for q in range(nb):
            write(q, lax.rem(g, owners) * pr, zag[q])

    finish(0)
    for d in range(1, ng):
        owner = lax.rem(g - d + ng, ng)

        @pl.when(owner < owners)
        def _(d=d, owner=owner):
            gag_copy(d).wait_recv()
            for q in range(nb):
                write(q, lax.rem(owner, owners) * pr, gag[d - 1, q])

    finish(1)

    for d in range(1, ng):
        deg_copy(d).wait_send()
        to, copy = wg_copy(d)
        pl.when(to < owners)(copy.wait_send)
        pl.when(g < owners)(gag_copy(d).wait_send)
    for h in range(HALVES):
        cot_copy(h, 0).wait_send()
        for d in range(2, ng, 2):
            cot_copy(h, d).wait_send()
            fwd_copy(h, d).wait_send()
    for d in range(1, nb):
        wz_copy(d).wait_send()
        for h in range(HALVES):
            part_copy(h, d).wait_send()
        pl.when(g < owners)(zag_copy(d).wait_send)


def outputs(pulled_b, w_sum, cot, w_self, w_neigh, gin, gself, gneigh):
    dims = (((1,), (1,)), ((), ()))
    width = cot.shape[1]
    own = lax.dot_general(cot[...], w_self[...], dims, preferred_element_type=F32)
    neigh = lax.dot_general(pulled_b[...], w_neigh[...], dims, preferred_element_type=F32)
    gin[...] = (own + neigh).astype(BF16)
    gself[...] = w_sum[:width, :].astype(F32)
    gneigh[...] = w_sum[width:, :].astype(F32)


def on_device(nb, ng, node_feats, mean_feats, cotangent, w_self, w_neigh, degree, adjacency, dst_tiles, src_tiles, tile_counts):
    rows, width = cotangent.shape
    tile, slots = adjacency.shape[-1], adjacency.shape[3]
    dev_tiles = rows // tile
    half = width // HALVES
    rq = 2 * width // nb
    pr = max(16, rq // ng)
    owners = rq // pr
    dims = (ng, nb, tile, slots, dev_tiles, rows, width, rq, pr, owners)
    any_spec = pl.BlockSpec(memory_space=pl.ANY)
    vmem, smem = pl.BlockSpec(memory_space=pltpu.VMEM), pl.BlockSpec(memory_space=pltpu.SMEM)
    dma = pltpu.SemaphoreType.DMA
    V = pltpu.VMEM
    pulled_b, w_sum = pl.pallas_call(
        functools.partial(kernel, dims),
        out_shape=(
            jax.ShapeDtypeStruct((rows, width), BF16),
            jax.ShapeDtypeStruct((2 * width, width), BF16),
        ),
        in_specs=[any_spec] * 3 + [vmem, any_spec] + [smem] * 3,
        out_specs=(vmem, vmem),
        scratch_shapes=[
            V((rows, width), BF16), V((rows, width), BF16), V((rows, width), BF16),
            V(adjacency.shape, BF16),
            V((ng, rows, half), BF16), V((ng, rows, half), BF16),
            V((ng - 1, dev_tiles, tile), jnp.int32),
            V((ng * dev_tiles, tile, width), BF16), V((ng * dev_tiles, tile, width), BF16),
            V((nb, rows, slots * tile), BF16),
            V((nb - 1, rows, half), BF16), V((nb - 1, rows, half), BF16),
            V((nb - 1, rows, half), BF16), V((nb - 1, rows, half), BF16),
            V((rows, half), F32), V((rows, half), F32), V((HALVES, rows, half), BF16),
            V((2 * width, width), F32), V((2 * width, width), BF16), V((nb - 1, rq, width), BF16),
            V((rq, width), F32), V((ng - 1, pr, width), F32),
            V((nb, pr, width), BF16), V((ng - 1, nb, pr, width), BF16),
            dma((4,)),
            dma((HALVES, 2, ng // 2)), dma((HALVES, ng)), dma((ng - 1,)), dma((ng - 1,)),
            dma((HALVES, nb - 1)), dma((HALVES, nb - 1)), dma((HALVES,)), dma((nb - 1,)), dma((nb - 1,)),
            dma((ng - 1,)), dma((ng - 1,)), dma((nb - 1,)), dma((nb - 1,)), dma((ng - 1,)), dma((ng - 1,)),
        ],
        compiler_params=pltpu.CompilerParams(
            collective_id=0, has_side_effects=True, vmem_limit_bytes=56 * 1024 * 1024
        ),
    )(
        cotangent, node_feats, mean_feats, degree.reshape(dev_tiles, tile),
        adjacency, dst_tiles, src_tiles, tile_counts,
    )
    return pl.pallas_call(
        outputs,
        out_shape=(
            jax.ShapeDtypeStruct((rows, width), BF16),
            jax.ShapeDtypeStruct((width, width), F32),
            jax.ShapeDtypeStruct((width, width), F32),
        ),
        in_specs=[vmem] * 5,
        out_specs=(vmem, vmem, vmem),
        compiler_params=pltpu.CompilerParams(vmem_limit_bytes=16 * 1024 * 1024),
    )(pulled_b, w_sum, cotangent, w_self, w_neigh)


def solution(mesh):
    placed = (
        P(("parts", "blk", "grp"), None),
        P(("parts", "blk", "grp"), None),
        P(("parts", "blk", "grp"), None),
        P(),
        P(),
        P(("parts", "blk", "grp")),
        P(("parts", "blk"), "grp", None, None, None, None),
        P(("parts", "blk"), "grp", None, None),
        P(("parts", "blk"), "grp", None, None),
        P(("parts", "blk"), "grp", None),
    )
    return jax.shard_map(
        functools.partial(on_device, mesh.shape["blk"], mesh.shape["grp"]),
        mesh=mesh,
        in_specs=placed,
        out_specs=(P(("parts", "blk", "grp"), None), P("parts", None), P("parts", None)),
        check_vma=False,
    )
```

```python
import functools

import jax
import jax.numpy as jnp
from jax import lax
from jax.experimental import pallas as pl
from jax.experimental.pallas import tpu as pltpu
from jax.sharding import PartitionSpec as P

MESH = pl.DeviceIdType.MESH
F32, BF16 = jnp.float32, jnp.bfloat16
HALVES = 2


def kernel(
    dims,
    cot, node, mean, deg, adj, dst, src, cnt,
    pulled_b, w_sum,
    cot_v, node_v, mean_v, adj_v,
    cot_in0, cot_in1, deg_in, scaled0, scaled1, placed,
    part_out0, part_out1, part_in0, part_in1, acc0, acc1, relay_in, held,
    w_acc, w_out, wz_in, wq, wg_in, zag, gag,
    load_sem, gs, gr, ds, dr, ps, pr_sem, rr, zs, zr, qs, qr, as_, ar, bs, br,
):
    ng, nb, tile, slots, dev_tiles, rows, width, rq, pr, owners = dims
    half = width // HALVES
    relay = nb >= 4
    g, b = lax.axis_index("grp"), lax.axis_index("blk")
    cot_in, scaled = (cot_in0, cot_in1), (scaled0, scaled1)
    part_out, part_in, acc = (part_out0, part_out1), (part_in0, part_in1), (acc0, acc1)

    loads = [
        pltpu.make_async_copy(a, v, load_sem.at[i])
        for i, (a, v) in enumerate(
            ((cot, cot_v), (node, node_v), (mean, mean_v), (adj, adj_v))
        )
    ]
    for c in loads:
        c.start()

    barrier = pltpu.get_barrier_semaphore()
    for d in range(1, ng):
        pl.semaphore_signal(barrier, inc=1, device_id={"grp": lax.rem(g + d, ng)}, device_id_type=MESH)
    for d in range(1, nb):
        pl.semaphore_signal(barrier, inc=1, device_id={"blk": lax.rem(b + d, nb)}, device_id_type=MESH)
    pl.semaphore_wait(barrier, ng - 1 + nb - 1)

    def deg_copy(d):
        return pltpu.make_async_remote_copy(
            src_ref=deg, dst_ref=deg_in.at[d - 1], send_sem=ds.at[d - 1], recv_sem=dr.at[d - 1],
            device_id={"grp": lax.rem(g + d, ng)}, device_id_type=MESH)

    sib = g + 1 - 2 * lax.rem(g, 2)

    def cot_copy(h, d):
        to = sib if d == 0 else lax.rem(g + d, ng)
        return pltpu.make_async_remote_copy(
            src_ref=cot_v.at[:, pl.ds(h * half, half)], dst_ref=cot_in[h].at[g],
            send_sem=gs.at[h, 0, d // 2], recv_sem=gr.at[h, g],
            device_id={"grp": to}, device_id_type=MESH)

    def fwd_copy(h, d):
        owner = lax.rem(g - d + ng, ng)
        return pltpu.make_async_remote_copy(
            src_ref=cot_in[h].at[owner], dst_ref=cot_in[h].at[owner],
            send_sem=gs.at[h, 1, d // 2], recv_sem=gr.at[h, owner],
            device_id={"grp": sib}, device_id_type=MESH)

    def cot_arrival(h, owner):
        return pltpu.make_async_remote_copy(
            src_ref=cot_in[h].at[owner], dst_ref=cot_in[h].at[owner],
            send_sem=gs.at[h, 0, 0], recv_sem=gr.at[h, owner],
            device_id={"grp": sib}, device_id_type=MESH)

    loads[0].wait()
    for d in range(1, ng):
        deg_copy(d).start()
    for d in range(2, ng, 2):
        cot_copy(0, d).start()
    cot_copy(0, 0).start()

    for c in loads[1:3]:
        c.wait()
    dims0 = (((0,), (0,)), ((), ()))
    for i, feats in enumerate((node_v, mean_v)):
        w = lax.dot_general(feats[...], cot_v[...], dims0, preferred_element_type=F32)
        w_acc[i * width:(i + 1) * width, :] = w
        w_out[i * width:(i + 1) * width, :] = w.astype(BF16)

    def wz_copy(d):
        to = lax.rem(b + d, nb)
        return pltpu.make_async_remote_copy(
            src_ref=w_out.at[pl.ds(pl.multiple_of(to * rq, rq), rq), :], dst_ref=wz_in.at[d - 1],
            send_sem=zs.at[d - 1], recv_sem=zr.at[d - 1],
            device_id={"blk": to}, device_id_type=MESH)

    for d in range(1, nb):
        wz_copy(d).start()

    loads[3].wait()

    def place(s, carry):
        for t in range(slots):
            turned = adj_v[0, 0, s, t].astype(F32).T
            live = t < cnt[0, 0, s]
            at = src[0, 0, s, t]
            for j in range(dev_tiles):
                keep = jnp.where(jnp.logical_and(live, at == j), 1.0, 0.0)
                placed[s, j * tile:(j + 1) * tile, t * tile:(t + 1) * tile] = (turned * keep).astype(BF16)
        return carry

    lax.fori_loop(0, nb, place, 0)

    eye = lax.broadcasted_iota(jnp.int32, (tile, tile), 0) == lax.broadcasted_iota(jnp.int32, (tile, tile), 1)

    def scale(h, owner, values, degrees):
        for k in range(dev_tiles):
            line = jnp.broadcast_to(degrees[k:k + 1, :].astype(F32), (tile, tile))
            inv = 1.0 / jnp.sum(jnp.where(eye, line, 0.0), axis=1, keepdims=True)
            x = values[k * tile:(k + 1) * tile, :].astype(F32) * inv
            hi = x.astype(BF16)
            lo = (x - hi.astype(F32)).astype(BF16)
            scaled[h][owner * dev_tiles + k, :, 0:half] = hi
            scaled[h][owner * dev_tiles + k, :, half:2 * half] = lo

    def partial(h, to):
        picked = jnp.concatenate([scaled[h][dst[0, 0, to, t]] for t in range(slots)], axis=0)
        both = jnp.dot(placed[to], picked, preferred_element_type=F32)
        return both[:, :half] + both[:, half:]

    def part_copy(h, d):
        return pltpu.make_async_remote_copy(
            src_ref=part_out[h].at[d - 1], dst_ref=part_in[h].at[d - 1],
            send_sem=ps.at[h, d - 1], recv_sem=pr_sem.at[h, d - 1],
            device_id={"blk": lax.rem(b + d, nb)}, device_id_type=MESH)

    def relay_copy(h, d):
        return pltpu.make_async_remote_copy(
            src_ref=part_out[h].at[d - 1], dst_ref=relay_in.at[h],
            send_sem=ps.at[h, d - 1], recv_sem=rr.at[h],
            device_id={"blk": 1 + (nb - 3) * (b // (nb - 1))}, device_id_type=MESH)

    def wg_copy(d):
        to = lax.rem(g + d, ng)
        at = lax.rem(to, owners)
        return to, pltpu.make_async_remote_copy(
            src_ref=wq.at[pl.ds(pl.multiple_of(at * pr, pr), pr), :], dst_ref=wg_in.at[d - 1],
            send_sem=qs.at[d - 1], recv_sem=qr.at[d - 1],
            device_id={"grp": to}, device_id_type=MESH)

    def zag_copy(d):
        return pltpu.make_async_remote_copy(
            src_ref=zag.at[b], dst_ref=zag.at[b], send_sem=as_.at[d - 1], recv_sem=ar.at[d - 1],
            device_id={"blk": lax.rem(b + d, nb)}, device_id_type=MESH)

    def gag_copy(d):
        return pltpu.make_async_remote_copy(
            src_ref=zag, dst_ref=gag.at[d - 1], send_sem=bs.at[d - 1], recv_sem=br.at[d - 1],
            device_id={"grp": lax.rem(g + d, ng)}, device_id_type=MESH)

    at_end = jnp.logical_or(b == 0, b == nb - 1)
    next_to_end = jnp.logical_or(b == 1, b == nb - 2)
    upper = b // (nb // 2)
    factor = (rows * nb * ng) ** (-0.5)

    def join_far(h):
        d = (nb - 2) * (1 - upper) + 2 * upper
        relay_copy(h, d).wait_recv()
        part_out[h][d - 1] = (held[h] + relay_in[h].astype(F32)).astype(BF16)
        part_copy(h, d).start()

    for h in range(HALVES):
        scale(h, g, cot_v[:, h * half:(h + 1) * half], deg[...])
        if h == 0:
            for d in range(1, ng):
                deg_copy(d).wait_recv()

        def arrived(owner, h=h):
            scale(h, owner, cot_in[h][owner], deg_in[lax.rem(g - owner + ng, ng) - 1])

        for d in range(2, ng, 2):
            cot_arrival(h, lax.rem(g - d + ng, ng)).wait_recv()
            fwd_copy(h, d).start()
        if h + 1 < HALVES:
            for d in range(2, ng, 2):
                cot_copy(h + 1, d).start()
            cot_copy(h + 1, 0).start()
        cot_arrival(h, sib).wait_recv()
        arrived(sib)
        for d in range(2, ng, 2):
            arrived(lax.rem(g - d + ng, ng))
        for d in range(2, ng, 2):
            owner = lax.rem(sib - d + ng, ng)
            cot_arrival(h, owner).wait_recv()
            arrived(owner)

        def send_part(i, carry, h=h):
            d = lax.rem(i + nb - 2, nb - 1) + 1
            d = d * (1 - 2 * upper) + nb * upper
            value = partial(h, lax.rem(b + d, nb))
            if not relay:
                part_out[h][d - 1] = value.astype(BF16)
                part_copy(h, d).start()
                return carry
            far = jnp.logical_and(at_end, i == 0)
            join = jnp.logical_and(next_to_end, i == nb - 2)

            @pl.when(join)
            def _():
                held[h] = value

            @pl.when(jnp.logical_not(join))
            def _():
                part_out[h][d - 1] = value.astype(BF16)

            @pl.when(far)
            def _():
                relay_copy(h, d).start()

            @pl.when(jnp.logical_not(jnp.logical_or(far, join)))
            def _():
                part_copy(h, d).start()

            return carry

        if h == 1:
            @pl.when(g < owners)
            def _():
                total = wq[pl.ds(pl.multiple_of(lax.rem(g, owners) * pr, pr), pr), :]
                for d in range(1, ng):
                    wg_copy(d)[1].wait_recv()
                    total = total + wg_in[d - 1]
                zag[b] = (total * factor).astype(BF16)
                for d in range(1, nb):
                    zag_copy(d).start()

        if relay and h == 1:
            pl.when(next_to_end)(functools.partial(join_far, 0))
        lax.fori_loop(0, nb - 1, send_part, 0)
        acc[h][...] = partial(h, b)

        if h == 0:
            total = w_acc[pl.ds(pl.multiple_of(b * rq, rq), rq), :]
            for d in range(1, nb):
                wz_copy(d).wait_recv()
                total = total + wz_in[d - 1].astype(F32)
            wq[...] = total
            for d in range(1, ng):
                to, copy = wg_copy(d)
                pl.when(to < owners)(copy.start)

    if relay:
        pl.when(next_to_end)(functools.partial(join_far, 1))

    def write(q, first, values):
        w_sum[pl.ds(pl.multiple_of(q * rq + first, pr), pr), :] = values

    def finish(h):
        for d in range(1, nb):
            def add(d=d):
                part_copy(h, d).wait_recv()
                acc[h][...] += part_in[h][d - 1].astype(F32)

            if relay and d == 1:
                pl.when(b != 0)(add)
            elif relay and d == nb - 1:
                pl.when(b != nb - 1)(add)
            else:
                add()
        pulled_b[:, h * half:(h + 1) * half] = acc[h][...].astype(BF16)

    @pl.when(g < owners)
    def _():
        for d in range(1, nb):
            zag_copy(d).wait_recv()
        for d in range(1, ng):
            gag_copy(d).start()
        for q in range(nb):
            write(q, lax.rem(g, owners) * pr, zag[q])

    finish(0)
    for d in range(1, ng):
        owner = lax.rem(g - d + ng, ng)

        @pl.when(owner < owners)
        def _(d=d, owner=owner):
            gag_copy(d).wait_recv()
            for q in range(nb):
                write(q, lax.rem(owner, owners) * pr, gag[d - 1, q])

    finish(1)

    for d in range(1, ng):
        deg_copy(d).wait_send()
        to, copy = wg_copy(d)
        pl.when(to < owners)(copy.wait_send)
        pl.when(g < owners)(gag_copy(d).wait_send)
    for h in range(HALVES):
        cot_copy(h, 0).wait_send()
        for d in range(2, ng, 2):
            cot_copy(h, d).wait_send()
            fwd_copy(h, d).wait_send()
    for d in range(1, nb):
        wz_copy(d).wait_send()
        for h in range(HALVES):
            part_copy(h, d).wait_send()
        pl.when(g < owners)(zag_copy(d).wait_send)


def outputs(pulled_b, w_sum, cot, w_self, w_neigh, gin, gself, gneigh):
    dims = (((1,), (1,)), ((), ()))
    width = cot.shape[1]
    own = lax.dot_general(cot[...], w_self[...], dims, preferred_element_type=F32)
    neigh = lax.dot_general(pulled_b[...], w_neigh[...], dims, preferred_element_type=F32)
    gin[...] = (own + neigh).astype(BF16)
    gself[...] = w_sum[:width, :].astype(F32)
    gneigh[...] = w_sum[width:, :].astype(F32)


def on_device(nb, ng, node_feats, mean_feats, cotangent, w_self, w_neigh, degree, adjacency, dst_tiles, src_tiles, tile_counts):
    rows, width = cotangent.shape
    tile, slots = adjacency.shape[-1], adjacency.shape[3]
    dev_tiles = rows // tile
    half = width // HALVES
    rq = 2 * width // nb
    pr = max(16, rq // ng)
    owners = rq // pr
    dims = (ng, nb, tile, slots, dev_tiles, rows, width, rq, pr, owners)
    any_spec = pl.BlockSpec(memory_space=pl.ANY)
    vmem, smem = pl.BlockSpec(memory_space=pltpu.VMEM), pl.BlockSpec(memory_space=pltpu.SMEM)
    dma = pltpu.SemaphoreType.DMA
    V = pltpu.VMEM
    pulled_b, w_sum = pl.pallas_call(
        functools.partial(kernel, dims),
        out_shape=(
            jax.ShapeDtypeStruct((rows, width), BF16),
            jax.ShapeDtypeStruct((2 * width, width), BF16),
        ),
        in_specs=[any_spec] * 3 + [vmem, any_spec] + [smem] * 3,
        out_specs=(vmem, vmem),
        scratch_shapes=[
            V((rows, width), BF16), V((rows, width), BF16), V((rows, width), BF16),
            V(adjacency.shape, BF16),
            V((ng, rows, half), BF16), V((ng, rows, half), BF16),
            V((ng - 1, dev_tiles, tile), jnp.int32),
            V((ng * dev_tiles, tile, width), BF16), V((ng * dev_tiles, tile, width), BF16),
            V((nb, rows, slots * tile), BF16),
            V((nb - 1, rows, half), BF16), V((nb - 1, rows, half), BF16),
            V((nb - 1, rows, half), BF16), V((nb - 1, rows, half), BF16),
            V((rows, half), F32), V((rows, half), F32), V((HALVES, rows, half), BF16), V((HALVES, rows, half), F32),
            V((2 * width, width), F32), V((2 * width, width), BF16), V((nb - 1, rq, width), BF16),
            V((rq, width), F32), V((ng - 1, pr, width), F32),
            V((nb, pr, width), BF16), V((ng - 1, nb, pr, width), BF16),
            dma((4,)),
            dma((HALVES, 2, ng // 2)), dma((HALVES, ng)), dma((ng - 1,)), dma((ng - 1,)),
            dma((HALVES, nb - 1)), dma((HALVES, nb - 1)), dma((HALVES,)), dma((nb - 1,)), dma((nb - 1,)),
            dma((ng - 1,)), dma((ng - 1,)), dma((nb - 1,)), dma((nb - 1,)), dma((ng - 1,)), dma((ng - 1,)),
        ],
        compiler_params=pltpu.CompilerParams(
            collective_id=0, has_side_effects=True, vmem_limit_bytes=56 * 1024 * 1024
        ),
    )(
        cotangent, node_feats, mean_feats, degree.reshape(dev_tiles, tile),
        adjacency, dst_tiles, src_tiles, tile_counts,
    )
    return pl.pallas_call(
        outputs,
        out_shape=(
            jax.ShapeDtypeStruct((rows, width), BF16),
            jax.ShapeDtypeStruct((width, width), F32),
            jax.ShapeDtypeStruct((width, width), F32),
        ),
        in_specs=[vmem] * 5,
        out_specs=(vmem, vmem, vmem),
        compiler_params=pltpu.CompilerParams(vmem_limit_bytes=56 * 1024 * 1024),
    )(pulled_b, w_sum, cotangent, w_self, w_neigh)


def solution(mesh):
    placed = (
        P(("parts", "blk", "grp"), None),
        P(("parts", "blk", "grp"), None),
        P(("parts", "blk", "grp"), None),
        P(),
        P(),
        P(("parts", "blk", "grp")),
        P(("parts", "blk"), "grp", None, None, None, None),
        P(("parts", "blk"), "grp", None, None),
        P(("parts", "blk"), "grp", None, None),
        P(("parts", "blk"), "grp", None),
    )
    return jax.shard_map(
        functools.partial(on_device, mesh.shape["blk"], mesh.shape["grp"]),
        mesh=mesh,
        in_specs=placed,
        out_specs=(P(("parts", "blk", "grp"), None), P("parts", None), P("parts", None)),
        check_vma=False,
    )
```

```python
import functools

import jax
import jax.numpy as jnp
from jax import lax
from jax.experimental import pallas as pl
from jax.experimental.pallas import tpu as pltpu
from jax.sharding import PartitionSpec as P

MESH = pl.DeviceIdType.MESH
F32, BF16 = jnp.float32, jnp.bfloat16
HALVES = 2


def kernel(
    dims,
    cot, node, mean, deg, adj, dst, src, cnt,
    pulled_b, w_sum,
    cot_v, node_v, mean_v, adj_v,
    cot_in0, cot_in1, deg_in, scaled0, scaled1, placed,
    part_out0, part_out1, part_in0, part_in1, acc0, acc1, relay_in, held,
    w_acc, w_out, wz_in, wq, wg_in, zag, gag,
    load_sem, gs, gr, ds, dr, ps, pr_sem, rr, zs, zr, qs, qr, as_, ar, bs, br,
):
    ng, nb, tile, slots, dev_tiles, rows, width, rq, pr, owners = dims
    half = width // HALVES
    relay = nb >= 4
    g, b = lax.axis_index("grp"), lax.axis_index("blk")
    cot_in, scaled = (cot_in0, cot_in1), (scaled0, scaled1)
    part_out, part_in, acc = (part_out0, part_out1), (part_in0, part_in1), (acc0, acc1)

    loads = [
        pltpu.make_async_copy(a, v, load_sem.at[i])
        for i, (a, v) in enumerate(
            ((cot, cot_v), (node, node_v), (mean, mean_v), (adj, adj_v))
        )
    ]
    for c in loads:
        c.start()

    barrier = pltpu.get_barrier_semaphore()
    for d in range(1, ng):
        pl.semaphore_signal(barrier, inc=1, device_id={"grp": lax.rem(g + d, ng)}, device_id_type=MESH)
    for d in range(1, nb):
        pl.semaphore_signal(barrier, inc=1, device_id={"blk": lax.rem(b + d, nb)}, device_id_type=MESH)
    pl.semaphore_wait(barrier, ng - 1 + nb - 1)

    def deg_copy(d):
        return pltpu.make_async_remote_copy(
            src_ref=deg, dst_ref=deg_in.at[d - 1], send_sem=ds.at[d - 1], recv_sem=dr.at[d - 1],
            device_id={"grp": lax.rem(g + d, ng)}, device_id_type=MESH)

    sib = g + 1 - 2 * lax.rem(g, 2)

    def cot_copy(h, d):
        to = sib if d == 0 else lax.rem(g + d, ng)
        return pltpu.make_async_remote_copy(
            src_ref=cot_v.at[:, pl.ds(h * half, half)], dst_ref=cot_in[h].at[g],
            send_sem=gs.at[h, 0, d // 2], recv_sem=gr.at[h, g],
            device_id={"grp": to}, device_id_type=MESH)

    def fwd_copy(h, d):
        owner = lax.rem(g - d + ng, ng)
        return pltpu.make_async_remote_copy(
            src_ref=cot_in[h].at[owner], dst_ref=cot_in[h].at[owner],
            send_sem=gs.at[h, 1, d // 2], recv_sem=gr.at[h, owner],
            device_id={"grp": sib}, device_id_type=MESH)

    def cot_arrival(h, owner):
        return pltpu.make_async_remote_copy(
            src_ref=cot_in[h].at[owner], dst_ref=cot_in[h].at[owner],
            send_sem=gs.at[h, 0, 0], recv_sem=gr.at[h, owner],
            device_id={"grp": sib}, device_id_type=MESH)

    loads[0].wait()
    for d in range(1, ng):
        deg_copy(d).start()
    for d in range(2, ng, 2):
        cot_copy(0, d).start()
    cot_copy(0, 0).start()

    for c in loads[1:3]:
        c.wait()
    dims0 = (((0,), (0,)), ((), ()))
    for i, feats in enumerate((node_v, mean_v)):
        w = lax.dot_general(feats[...], cot_v[...], dims0, preferred_element_type=F32)
        w_acc[i * width:(i + 1) * width, :] = w
        w_out[i * width:(i + 1) * width, :] = w.astype(BF16)

    def wz_copy(d):
        to = lax.rem(b + d, nb)
        return pltpu.make_async_remote_copy(
            src_ref=w_out.at[pl.ds(pl.multiple_of(to * rq, rq), rq), :], dst_ref=wz_in.at[d - 1],
            send_sem=zs.at[d - 1], recv_sem=zr.at[d - 1],
            device_id={"blk": to}, device_id_type=MESH)

    for d in range(1, nb):
        wz_copy(d).start()

    loads[3].wait()

    def place(s, carry):
        for t in range(slots):
            turned = adj_v[0, 0, s, t].astype(F32).T
            live = t < cnt[0, 0, s]
            at = src[0, 0, s, t]
            for j in range(dev_tiles):
                keep = jnp.where(jnp.logical_and(live, at == j), 1.0, 0.0)
                placed[s, j * tile:(j + 1) * tile, t * tile:(t + 1) * tile] = (turned * keep).astype(BF16)
        return carry

    lax.fori_loop(0, nb, place, 0)

    eye = lax.broadcasted_iota(jnp.int32, (tile, tile), 0) == lax.broadcasted_iota(jnp.int32, (tile, tile), 1)

    def scale(h, owner, values, degrees):
        for k in range(dev_tiles):
            line = jnp.broadcast_to(degrees[k:k + 1, :].astype(F32), (tile, tile))
            inv = 1.0 / jnp.sum(jnp.where(eye, line, 0.0), axis=1, keepdims=True)
            x = values[k * tile:(k + 1) * tile, :].astype(F32) * inv
            hi = x.astype(BF16)
            lo = (x - hi.astype(F32)).astype(BF16)
            scaled[h][owner * dev_tiles + k, :, 0:half] = hi
            scaled[h][owner * dev_tiles + k, :, half:2 * half] = lo

    def partial(h, to):
        picked = jnp.concatenate([scaled[h][dst[0, 0, to, t]] for t in range(slots)], axis=0)
        both = jnp.dot(placed[to], picked, preferred_element_type=F32)
        return both[:, :half] + both[:, half:]

    def part_copy(h, d):
        return pltpu.make_async_remote_copy(
            src_ref=part_out[h].at[d - 1], dst_ref=part_in[h].at[d - 1],
            send_sem=ps.at[h, d - 1], recv_sem=pr_sem.at[h, d - 1],
            device_id={"blk": lax.rem(b + d, nb)}, device_id_type=MESH)

    def relay_copy(h, d):
        return pltpu.make_async_remote_copy(
            src_ref=part_out[h].at[d - 1], dst_ref=relay_in.at[h],
            send_sem=ps.at[h, d - 1], recv_sem=rr.at[h],
            device_id={"blk": 1 + (nb - 3) * (b // (nb - 1))}, device_id_type=MESH)

    def wg_copy(d):
        to = lax.rem(g + d, ng)
        at = lax.rem(to, owners)
        return to, pltpu.make_async_remote_copy(
            src_ref=wq.at[pl.ds(pl.multiple_of(at * pr, pr), pr), :], dst_ref=wg_in.at[d - 1],
            send_sem=qs.at[d - 1], recv_sem=qr.at[d - 1],
            device_id={"grp": to}, device_id_type=MESH)

    def zag_copy(d):
        return pltpu.make_async_remote_copy(
            src_ref=zag.at[b], dst_ref=zag.at[b], send_sem=as_.at[d - 1], recv_sem=ar.at[d - 1],
            device_id={"blk": lax.rem(b + d, nb)}, device_id_type=MESH)

    def gag_copy(d):
        return pltpu.make_async_remote_copy(
            src_ref=zag, dst_ref=gag.at[d - 1], send_sem=bs.at[d - 1], recv_sem=br.at[d - 1],
            device_id={"grp": lax.rem(g + d, ng)}, device_id_type=MESH)

    at_end = jnp.logical_or(b == 0, b == nb - 1)
    next_to_end = jnp.logical_or(b == 1, b == nb - 2)
    upper = b // (nb // 2)
    factor = (rows * nb * ng) ** (-0.5)

    def join_far(h):
        d = (nb - 2) * (1 - upper) + 2 * upper
        relay_copy(h, d).wait_recv()
        part_out[h][d - 1] = (held[h] + relay_in[h].astype(F32)).astype(BF16)
        part_copy(h, d).start()

    for h in range(HALVES):
        scale(h, g, cot_v[:, h * half:(h + 1) * half], deg[...])
        if h == 0:
            for d in range(1, ng):
                deg_copy(d).wait_recv()

        def arrived(owner, h=h):
            scale(h, owner, cot_in[h][owner], deg_in[lax.rem(g - owner + ng, ng) - 1])

        for d in range(2, ng, 2):
            cot_arrival(h, lax.rem(g - d + ng, ng)).wait_recv()
            fwd_copy(h, d).start()
        if h + 1 < HALVES:
            for d in range(2, ng, 2):
                cot_copy(h + 1, d).start()
            cot_copy(h + 1, 0).start()
        cot_arrival(h, sib).wait_recv()
        arrived(sib)
        for d in range(2, ng, 2):
            arrived(lax.rem(g - d + ng, ng))
        for d in range(2, ng, 2):
            owner = lax.rem(sib - d + ng, ng)
            cot_arrival(h, owner).wait_recv()
            arrived(owner)

        def send_part(i, carry, h=h):
            d = lax.rem(i + nb - 2, nb - 1) + 1
            d = d * (1 - 2 * upper) + nb * upper
            value = partial(h, lax.rem(b + d, nb))
            if not relay:
                part_out[h][d - 1] = value.astype(BF16)
                part_copy(h, d).start()
                return carry
            far = jnp.logical_and(at_end, i == 0)
            join = jnp.logical_and(next_to_end, i == nb - 2)

            @pl.when(join)
            def _():
                held[h] = value

            @pl.when(jnp.logical_not(join))
            def _():
                part_out[h][d - 1] = value.astype(BF16)

            @pl.when(far)
            def _():
                relay_copy(h, d).start()

            @pl.when(jnp.logical_not(jnp.logical_or(far, join)))
            def _():
                part_copy(h, d).start()

            return carry

        if h == 1:
            @pl.when(g < owners)
            def _():
                total = wq[pl.ds(pl.multiple_of(lax.rem(g, owners) * pr, pr), pr), :]
                for d in range(1, ng):
                    wg_copy(d)[1].wait_recv()
                    total = total + wg_in[d - 1]
                zag[b] = (total * factor).astype(BF16)
                for d in range(1, nb):
                    zag_copy(d).start()

        if relay and h == 1:
            pl.when(next_to_end)(functools.partial(join_far, 0))
        lax.fori_loop(0, nb - 1, send_part, 0)
        acc[h][...] = partial(h, b)

        if h == 0:
            total = w_acc[pl.ds(pl.multiple_of(b * rq, rq), rq), :]
            for d in range(1, nb):
                wz_copy(d).wait_recv()
                total = total + wz_in[d - 1].astype(F32)
            wq[...] = total
            for d in range(1, ng):
                to, copy = wg_copy(d)
                pl.when(to < owners)(copy.start)

    if relay:
        pl.when(next_to_end)(functools.partial(join_far, 1))

    def write(q, first, values):
        w_sum[pl.ds(pl.multiple_of(q * rq + first, pr), pr), :] = values

    def finish(h):
        for d in range(1, nb):
            def add(d=d):
                part_copy(h, d).wait_recv()
                acc[h][...] += part_in[h][d - 1].astype(F32)

            if relay and d == 1:
                pl.when(b != 0)(add)
            elif relay and d == nb - 1:
                pl.when(b != nb - 1)(add)
            else:
                add()
        pulled_b[:, h * half:(h + 1) * half] = acc[h][...].astype(BF16)

    @pl.when(g < owners)
    def _():
        for d in range(1, nb):
            zag_copy(d).wait_recv()
        for d in range(1, ng):
            gag_copy(d).start()
        for q in range(nb):
            write(q, lax.rem(g, owners) * pr, zag[q])

    finish(0)
    for d in range(1, ng):
        owner = lax.rem(g - d + ng, ng)

        @pl.when(owner < owners)
        def _(d=d, owner=owner):
            gag_copy(d).wait_recv()
            for q in range(nb):
                write(q, lax.rem(owner, owners) * pr, gag[d - 1, q])

    finish(1)

    for d in range(1, ng):
        deg_copy(d).wait_send()
        to, copy = wg_copy(d)
        pl.when(to < owners)(copy.wait_send)
        pl.when(g < owners)(gag_copy(d).wait_send)
    for h in range(HALVES):
        cot_copy(h, 0).wait_send()
        for d in range(2, ng, 2):
            cot_copy(h, d).wait_send()
            fwd_copy(h, d).wait_send()
    for d in range(1, nb):
        wz_copy(d).wait_send()
        for h in range(HALVES):
            part_copy(h, d).wait_send()
        pl.when(g < owners)(zag_copy(d).wait_send)


def outputs(pulled_b, w_sum, cot, w_self, w_neigh, gin, gself, gneigh, pv, wv, cv, sv, nv, gv, selfv, neighv, isem, osem):
    dims = (((1,), (1,)), ((), ()))
    width = cot.shape[1]
    loads = [
        pltpu.make_async_copy(x, v, isem.at[i])
        for i, (x, v) in enumerate(((w_sum, wv), (cot, cv), (w_self, sv), (pulled_b, pv), (w_neigh, nv)))
    ]
    stores = [
        pltpu.make_async_copy(v, x, osem.at[i])
        for i, (v, x) in enumerate(((selfv, gself), (neighv, gneigh), (gv, gin)))
    ]
    for c in loads:
        c.start()
    loads[0].wait()
    selfv[...] = wv[:width, :].astype(F32)
    stores[0].start()
    neighv[...] = wv[width:, :].astype(F32)
    stores[1].start()
    for c in loads[1:]:
        c.wait()
    own = lax.dot_general(cv[...], sv[...], dims, preferred_element_type=F32)
    neigh = lax.dot_general(pv[...], nv[...], dims, preferred_element_type=F32)
    gv[...] = (own + neigh).astype(BF16)
    stores[2].start()
    for c in stores:
        c.wait()


def on_device(nb, ng, node_feats, mean_feats, cotangent, w_self, w_neigh, degree, adjacency, dst_tiles, src_tiles, tile_counts):
    rows, width = cotangent.shape
    tile, slots = adjacency.shape[-1], adjacency.shape[3]
    dev_tiles = rows // tile
    half = width // HALVES
    rq = 2 * width // nb
    pr = max(16, rq // ng)
    owners = rq // pr
    dims = (ng, nb, tile, slots, dev_tiles, rows, width, rq, pr, owners)
    any_spec = pl.BlockSpec(memory_space=pl.ANY)
    vmem, smem = pl.BlockSpec(memory_space=pltpu.VMEM), pl.BlockSpec(memory_space=pltpu.SMEM)
    dma = pltpu.SemaphoreType.DMA
    V = pltpu.VMEM
    pulled_b, w_sum = pl.pallas_call(
        functools.partial(kernel, dims),
        out_shape=(
            jax.ShapeDtypeStruct((rows, width), BF16),
            jax.ShapeDtypeStruct((2 * width, width), BF16),
        ),
        in_specs=[any_spec] * 3 + [vmem, any_spec] + [smem] * 3,
        out_specs=(vmem, vmem),
        scratch_shapes=[
            V((rows, width), BF16), V((rows, width), BF16), V((rows, width), BF16),
            V(adjacency.shape, BF16),
            V((ng, rows, half), BF16), V((ng, rows, half), BF16),
            V((ng - 1, dev_tiles, tile), jnp.int32),
            V((ng * dev_tiles, tile, width), BF16), V((ng * dev_tiles, tile, width), BF16),
            V((nb, rows, slots * tile), BF16),
            V((nb - 1, rows, half), BF16), V((nb - 1, rows, half), BF16),
            V((nb - 1, rows, half), BF16), V((nb - 1, rows, half), BF16),
            V((rows, half), F32), V((rows, half), F32), V((HALVES, rows, half), BF16), V((HALVES, rows, half), F32),
            V((2 * width, width), F32), V((2 * width, width), BF16), V((nb - 1, rq, width), BF16),
            V((rq, width), F32), V((ng - 1, pr, width), F32),
            V((nb, pr, width), BF16), V((ng - 1, nb, pr, width), BF16),
            dma((4,)),
            dma((HALVES, 2, ng // 2)), dma((HALVES, ng)), dma((ng - 1,)), dma((ng - 1,)),
            dma((HALVES, nb - 1)), dma((HALVES, nb - 1)), dma((HALVES,)), dma((nb - 1,)), dma((nb - 1,)),
            dma((ng - 1,)), dma((ng - 1,)), dma((nb - 1,)), dma((nb - 1,)), dma((ng - 1,)), dma((ng - 1,)),
        ],
        compiler_params=pltpu.CompilerParams(
            collective_id=0, has_side_effects=True, vmem_limit_bytes=56 * 1024 * 1024
        ),
    )(
        cotangent, node_feats, mean_feats, degree.reshape(dev_tiles, tile),
        adjacency, dst_tiles, src_tiles, tile_counts,
    )
    return pl.pallas_call(
        outputs,
        out_shape=(
            jax.ShapeDtypeStruct((rows, width), BF16),
            jax.ShapeDtypeStruct((width, width), F32),
            jax.ShapeDtypeStruct((width, width), F32),
        ),
        in_specs=[any_spec] * 5,
        out_specs=(any_spec, any_spec, any_spec),
        scratch_shapes=[
            V((rows, width), BF16), V((2 * width, width), BF16), V((rows, width), BF16),
            V((width, width), BF16), V((width, width), BF16), V((rows, width), BF16),
            V((width, width), F32), V((width, width), F32), dma((5,)), dma((3,)),
        ],
        compiler_params=pltpu.CompilerParams(vmem_limit_bytes=56 * 1024 * 1024),
    )(pulled_b, w_sum, cotangent, w_self, w_neigh)


def solution(mesh):
    placed = (
        P(("parts", "blk", "grp"), None),
        P(("parts", "blk", "grp"), None),
        P(("parts", "blk", "grp"), None),
        P(),
        P(),
        P(("parts", "blk", "grp")),
        P(("parts", "blk"), "grp", None, None, None, None),
        P(("parts", "blk"), "grp", None, None),
        P(("parts", "blk"), "grp", None, None),
        P(("parts", "blk"), "grp", None),
    )
    return jax.shard_map(
        functools.partial(on_device, mesh.shape["blk"], mesh.shape["grp"]),
        mesh=mesh,
        in_specs=placed,
        out_specs=(P(("parts", "blk", "grp"), None), P("parts", None), P("parts", None)),
        check_vma=False,
    )
```
